32 devices in a mesh: rows: 8 (over z, y), feat: 4 (over x, core).
Axes of the slice: x: 2, y: 2, z: 4, core: 2. Of those that a mesh axis runs over, the one named last changes fastest.
Arguments:
- bin_codes: int32 [16, 122880], P(None, 'rows'), may hold values from 0 to 255
- node_ids: int32 [122880], P('rows'), may hold values from 0 to 7, as said below
- labels: float32 [122880], P('rows'), may hold values from -1 to 1, as said below
- weights: float32 [122880], P('rows'), as said below
- predictions: float32 [122880], P('rows'), may hold values from -6 to 6
- level3_feature: int32 [8], replicated, may hold values from 0 to 15
- level3_bin: int32 [8], replicated, may hold values from 64 to 191
- level4_feature: int32 [16], replicated, may hold values from 0 to 15
- level4_bin: int32 [16], replicated, may hold values from 64 to 191
Outputs:
- level3_hist: float32 [16, 16, 256], P('feat')
- level4_hist: float32 [16, 32, 256], P('feat')
- leaf_values: float32 [32], replicated
- new_predictions: float32 [122880], P('rows')
- new_weights: float32 [122880], P('rows')
The draws below stay inside these ranges and needn't reach their ends.
Inputs may be any that keep to these rules, and one draw needn't show every extreme that they name: `node_ids`: node ids of level 3. `labels`: every label is -1 or 1. `weights`: every weight is positive.
All inputs are finite; a program needn't handle non-finite values.
Results may differ from the reference program's by a relative error of at most 0.0003.
Values sent between devices are 32-bit elements; how exact they have to be, the bound alone decides.
No kernel may reach another device: no remote copies, remote signals or barrier semaphores. Data moves between devices by JAX's collectives and lax.ppermute only.
A program may use at most 64 MiB of HBM per device.

```python
import jax
import jax.numpy as jnp
from jax import lax

FEATURES = 16
BINS = 256
NODES3 = 8
NODES4 = 16
LEAVES = 32
ROWS = 122880


def joint_rows(key):
    node_of = jax.random.randint(jax.random.fold_in(key, 11), (ROWS,), 0, NODES3)
    tilted = jax.random.uniform(jax.random.fold_in(key, 12), (NODES3,), minval=0.1, maxval=0.9)
    chance = jax.random.uniform(jax.random.fold_in(key, 13), (ROWS,))
    label_row = jnp.where(chance < tilted[node_of], 1.0, -1.0).astype(jnp.float32)
    return (node_of, label_row)


def draw_node_ids(key, part):
    return joint_rows(key)[0]


def draw_labels(key, part):
    return joint_rows(key)[1]


def draw_weights(key, part):
    position = jnp.arange(ROWS, dtype=jnp.float32) / ROWS
    ramped = 1.0 + 2.0 * position
    lowest = 0.2
    spread = jnp.exp(jax.random.uniform(jax.random.fold_in(key, 21), (ROWS,), minval=jnp.log(lowest), maxval=jnp.log(2.0)))
    return (ramped * spread * (NODES3 * BINS / ROWS)).astype(jnp.float32)


def touch_ends(entries, stream_key, least, top_value):
    longest = entries.shape.index(max(entries.shape))
    spots = []
    for shift in (0, 1):
        where = [jax.random.randint(jax.random.fold_in(stream_key, axis), (), 0, length) for axis, length in enumerate(entries.shape)]
        where[longest] = (where[longest] + shift) % entries.shape[longest]
        spots.append(tuple(where))
    return entries.at[spots[0]].set(least).at[spots[1]].set(top_value)


def shard_levels(rng, extent, split, smallest, high):
    loudness = 1.0
    for dim, shards_of in split:
        draws = jax.random.uniform(jax.random.fold_in(jax.random.fold_in(rng, 6), dim), (shards_of,), jnp.float32, smallest / len(split), high / len(split))
        loudness = loudness * jnp.repeat(jnp.exp(draws), extent[dim] // shards_of).reshape((-1,) + (1,) * (len(extent) - 1 - dim))
    return loudness


def gaussian(rng, shape, width, reach, cuts=(), held_as=jnp.bfloat16):
    values = jax.random.normal(rng, shape, jnp.float32) * width
    if len(cuts) > 0:
        values = shard_levels(rng, shape, cuts, -0.22, 0.18) * values
    return jnp.clip(values, min=-reach, max=reach).astype(held_as)


def setup_inputs(seed: int = 0) -> dict:
    key_list = jax.random.split(jax.random.key(seed), 10)
    bin_codes = touch_ends(jax.random.randint(key_list[0], (FEATURES, ROWS), 0, BINS), jax.random.fold_in(key_list[0], 1), 0, BINS - 1).astype(jnp.int32)
    node_ids = draw_node_ids(jax.random.fold_in(key_list[9], 71), 0)
    labels = draw_labels(jax.random.fold_in(key_list[9], 71), 0)
    weights = draw_weights(jax.random.fold_in(key_list[9], 71), 0)
    predictions = gaussian(key_list[4], (ROWS,), 1.0, 6.0, ((0, 8),), jnp.float32)
    level3_feature = touch_ends(jax.random.randint(key_list[5], (NODES3,), 0, FEATURES), jax.random.fold_in(key_list[5], 1), 0, FEATURES - 1).astype(jnp.int32)
    level3_bin = touch_ends(jax.random.randint(key_list[6], (NODES3,), BINS // 4, 3 * BINS // 4), jax.random.fold_in(key_list[6], 1), BINS // 4, (3 * BINS // 4) - 1).astype(jnp.int32)
    level4_feature = touch_ends(jax.random.randint(key_list[7], (NODES4,), 0, FEATURES), jax.random.fold_in(key_list[7], 1), 0, FEATURES - 1).astype(jnp.int32)
    level4_bin = touch_ends(jax.random.randint(key_list[8], (NODES4,), BINS // 4, 3 * BINS // 4), jax.random.fold_in(key_list[8], 1), BINS // 4, (3 * BINS // 4) - 1).astype(jnp.int32)
    return {"bin_codes": bin_codes, "node_ids": node_ids, "labels": labels, "weights": weights, "predictions": predictions, "level3_feature": level3_feature, "level3_bin": level3_bin, "level4_feature": level4_feature, "level4_bin": level4_bin}


def rounded(values):
    return lax.optimization_barrier(values.astype(jnp.bfloat16)).astype(jnp.float32)


def histogram(bin_codes, node_of, node_count, weight_round, signed_round):
    def one_feature(code_row):
        slot = node_of * BINS + code_row
        weight_sums = jax.ops.segment_sum(weight_round, slot, num_segments=node_count * BINS)
        signed_sums = jax.ops.segment_sum(signed_round, slot, num_segments=node_count * BINS)
        return jnp.concatenate([weight_sums.reshape(node_count, BINS), signed_sums.reshape(node_count, BINS)], axis=0)
    return lax.map(one_feature, bin_codes)


def routing(bin_codes, node_of, features, thresholds):
    chosen = features[node_of]
    cutoff = thresholds[node_of]
    picked = bin_codes[chosen, jnp.arange(node_of.shape[0], dtype=jnp.int32)]
    return (picked > cutoff).astype(jnp.int32)


def reference(bin_codes, node_ids, labels, weights, predictions, level3_feature, level3_bin, level4_feature, level4_bin):
    weight_round = rounded(weights)
    signed_round = rounded(weights * labels)
    level3_hist = histogram(bin_codes, node_ids, NODES3, weight_round, signed_round)
    node_four = 2 * node_ids + routing(bin_codes, node_ids, level3_feature, level3_bin)
    level4_hist = histogram(bin_codes, node_four, NODES4, weight_round, signed_round)
    leaf_of = 2 * node_four + routing(bin_codes, node_four, level4_feature, level4_bin)
    leaf_weight = jax.ops.segment_sum(weight_round, leaf_of, num_segments=LEAVES)
    leaf_signed = jax.ops.segment_sum(signed_round, leaf_of, num_segments=LEAVES)
    leaf_values = leaf_signed / (leaf_weight + 1.0)
    stepped = leaf_values[leaf_of]
    new_predictions = predictions + stepped
    raw_weights = weights * jnp.exp(-labels * stepped)
    new_weights = raw_weights * (ROWS / jnp.sum(raw_weights))
    return (level3_hist, level4_hist, leaf_values, new_predictions, new_weights)
```

```python
import functools

import jax
import jax.numpy as jnp
from jax import lax
from jax.experimental import pallas as pl
from jax.experimental.pallas import tpu as pltpu
from jax.sharding import PartitionSpec as P

BINS = 256
LANES = 128
SUB = 8
NT = (((1,), (1,)), ((), ()))


def grow_kernel(
    own_ref,
    f3_ref,
    b3_ref,
    f4_ref,
    b4_ref,
    codes_ref,
    node_ref,
    label_ref,
    weight_ref,
    hist_ref,
    path_ref,
    low_ref,
    slot_ref,
    high_ref,
    mid_ref,
    rest_ref,
):
    groups = node_ref.shape[0]
    steps = groups // SUB
    own = low_ref.shape[0]
    nodes3 = f3_ref.shape[0]
    nodes4 = f4_ref.shape[0]
    tag_count = 2 * nodes4
    paths = 4 * nodes4

    def code_block(feature, step):
        start = (feature // SUB) * (groups * SUB) + step * (SUB * SUB) + feature % SUB
        return codes_ref[pl.ds(start, SUB, stride=SUB), :]

    def route(step, carry):
        rows = pl.ds(step * SUB, SUB)
        node = node_ref[rows, :]
        positive = jnp.where(label_ref[rows, :] > 0, 1, 0)
        weight = weight_ref[rows, :]
        right3 = jnp.zeros((SUB, LANES), jnp.int32)
        for n in range(nodes3):
            above = jnp.where(code_block(f3_ref[n], step) > b3_ref[n], 1, 0)
            right3 = jnp.where(node == n, above, right3)
        node4 = 2 * node + right3
        right4 = jnp.zeros((SUB, LANES), jnp.int32)
        for n in range(nodes4):
            above = jnp.where(code_block(f4_ref[n], step) > b4_ref[n], 1, 0)
            right4 = jnp.where(node4 == n, above, right4)
        tag = right3 * (2 * nodes3) + positive * nodes3 + node
        path_ref[rows, :] = positive * (2 * nodes4) + 2 * node4 + right4
        for i in range(own):
            code = code_block(own_ref[0] + i, step)
            low_ref[i, rows, :] = code & (LANES - 1)
            slot_ref[i, rows, :] = (code // LANES) * tag_count + tag
        high = weight.astype(jnp.bfloat16).astype(jnp.float32)
        mid = (weight - high).astype(jnp.bfloat16).astype(jnp.float32)
        high_ref[rows, :] = high
        mid_ref[rows, :] = mid
        rest_ref[rows, :] = weight - high - mid
        return carry

    lax.fori_loop(0, steps, route, 0)
    hist_ref[...] = jnp.zeros_like(hist_ref)
    cell = (2 * SUB, LANES)
    iota = lax.broadcasted_iota(jnp.int32, cell, 0)
    small = jnp.int16
    ranks = [(iota + 2 * SUB * g).astype(small) for g in range(LANES // (2 * SUB))]
    one = jnp.ones(cell, jnp.bfloat16)
    nothing = jnp.zeros(cell, jnp.bfloat16)

    def spread(ref, row, dtype, *lead):
        line = ref[(*lead, pl.ds(row, 1), slice(None))]
        return jnp.broadcast_to(line, cell).astype(dtype)

    def onehot(value, count, filled):
        parts = [jnp.where(value == ranks[g], filled, nothing) for g in range(count // (2 * SUB))]
        return jnp.concatenate(parts, axis=0)

    def tally(step, carry):
        base = step * SUB
        lines = range(SUB)
        heavy = [spread(high_ref, base + k, jnp.bfloat16) for k in lines]
        for i in range(own):
            slots = jnp.concatenate(
                [
                    onehot(spread(slot_ref, base + k, small, i), 2 * tag_count, heavy[k])
                    for k in lines
                ],
                axis=1,
            )
            lows = jnp.concatenate(
                [onehot(spread(low_ref, base + k, small, i), LANES, one) for k in lines],
                axis=1,
            )
            part = pl.ds(i * 2 * tag_count, 2 * tag_count)
            hist_ref[part, :] += lax.dot_general(
                slots, lows, NT, preferred_element_type=jnp.float32
            )
        pieces = []
        for k in lines:
            mid = spread(mid_ref, base + k, jnp.bfloat16)
            rest = spread(rest_ref, base + k, jnp.bfloat16)
            pieces.append(
                jnp.where(
                    ranks[0] == 0,
                    heavy[k],
                    jnp.where(ranks[0] == 1, mid, jnp.where(ranks[0] == 2, rest, nothing)),
                )
            )
        trails = jnp.concatenate(
            [onehot(spread(path_ref, base + k, small), LANES, one) for k in lines], axis=1
        )
        part = pl.ds(own * 2 * tag_count, 2 * SUB)
        hist_ref[part, :] += lax.dot_general(
            jnp.concatenate(pieces, axis=1), trails, NT, preferred_element_type=jnp.float32
        )
        return carry

    lax.fori_loop(0, steps, tally, 0)


def finish_kernel(
    total,
    hist_ref,
    path_ref,
    label_ref,
    weight_ref,
    score_ref,
    hist3_ref,
    hist4_ref,
    value_ref,
    new_score_ref,
    new_weight_ref,
    weave_ref,
):
    own, rows4, _ = hist4_ref.shape
    tags = rows4
    nodes4 = tags // 2
    nodes3 = nodes4 // 2
    leaves = value_ref.shape[1]
    for i in range(own):
        base = i * 2 * tags
        for h in range(2):
            lanes = slice(h * LANES, (h + 1) * LANES)
            start = base + h * tags

            def tag_rows(right, positive):
                first = start + right * 2 * nodes3 + positive * nodes3
                return hist_ref[first : first + nodes3, :]

            sums = [tag_rows(r, 1) + tag_rows(r, 0) for r in range(2)]
            diffs = [tag_rows(r, 1) - tag_rows(r, 0) for r in range(2)]
            hist3_ref[i, 0:nodes3, lanes] = sums[0] + sums[1]
            hist3_ref[i, nodes3 : 2 * nodes3, lanes] = diffs[0] + diffs[1]
            for r in range(2):
                weave_ref[pl.ds(start + r, nodes3, stride=2), :] = sums[r]
                weave_ref[pl.ds(start + nodes4 + r, nodes3, stride=2), :] = diffs[r]
            hist4_ref[i, :, lanes] = weave_ref[start : start + tags, :]
    leaf_base = own * 2 * tags
    pieces = hist_ref[leaf_base : leaf_base + SUB, :]
    lane = lax.broadcasted_iota(jnp.int32, (1, LANES), 1)
    rounded = pieces[0:1, :]
    full = pieces[0:1, :] + (pieces[1:2, :] + pieces[2:3, :])
    other = pltpu.roll(rounded, LANES - leaves, 1)
    values = (other - rounded) / (other + rounded + 1.0)
    value_ref[...] = values[:, 0:leaves]
    negative = lane < leaves
    both = jnp.where(negative, values, pltpu.roll(values, leaves, 1))
    both = jnp.where(lane < 2 * leaves, both, 0.0)
    growth = jnp.exp(jnp.where(negative, both, -both))
    grand = jnp.sum(full * growth, axis=1, keepdims=True)
    factor = growth * (total / grand)
    factor8 = jnp.broadcast_to(factor, (SUB, LANES))
    both8 = jnp.broadcast_to(both, (SUB, LANES))
    for step in range(path_ref.shape[0] // SUB):
        rows = slice(step * SUB, (step + 1) * SUB)
        path = path_ref[rows, :]
        scale = jnp.take_along_axis(factor8, path, axis=1)
        shift = jnp.take_along_axis(both8, path, axis=1)
        new_weight_ref[rows, :] = weight_ref[rows, :] * scale
        new_score_ref[rows, :] = score_ref[rows, :] + shift


def combine_rows(part, axis, size):
    if size & (size - 1):
        return lax.psum(part, axis)
    reach = 1
    while reach < size:
        pairs = [(i, i ^ reach) for i in range(size)]
        part = part + lax.ppermute(part, axis, pairs)
        reach *= 2
    return part


def whole(memory=pltpu.VMEM):
    return pl.BlockSpec(memory_space=memory)


def on_device(
    row_parts,
    feat_parts,
    bin_codes,
    node_ids,
    labels,
    weights,
    predictions,
    level3_feature,
    level3_bin,
    level4_feature,
    level4_bin,
):
    features, row_count = bin_codes.shape
    groups = row_count // LANES
    own = features // feat_parts
    nodes3 = level3_feature.shape[0]
    nodes4 = level4_feature.shape[0]
    leaves = 2 * nodes4
    tags = 2 * nodes4
    first = (lax.axis_index("feat") * own).astype(jnp.int32).reshape(1)
    codes = (
        bin_codes.reshape(features // SUB, SUB, groups, LANES)
        .transpose(0, 2, 1, 3)
        .reshape(features * groups, LANES)
    )
    square = (groups, LANES)
    node_sq = node_ids.reshape(square)
    label_sq = labels.reshape(square)
    weight_sq = weights.reshape(square)
    score_sq = predictions.reshape(square)
    hist_rows = own * 2 * tags + 2 * SUB
    f32 = jnp.float32
    hist, path = pl.pallas_call(
        grow_kernel,
        out_shape=(
            jax.ShapeDtypeStruct((hist_rows, LANES), f32),
            jax.ShapeDtypeStruct(square, jnp.int32),
        ),
        in_specs=[whole(pltpu.SMEM)] * 5 + [whole()] * 4,
        out_specs=(whole(), whole()),
        scratch_shapes=[
            pltpu.VMEM((own, *square), jnp.int32),
            pltpu.VMEM((own, *square), jnp.int32),
            pltpu.VMEM(square, f32),
            pltpu.VMEM(square, f32),
            pltpu.VMEM(square, f32),
        ],
        compiler_params=pltpu.CompilerParams(vmem_limit_bytes=24 * 1024 * 1024),
    )(first, level3_feature, level3_bin, level4_feature, level4_bin, codes, node_sq, label_sq, weight_sq)
    hist = combine_rows(hist, "rows", row_parts)
    hist3, hist4, values, new_scores, new_weights = pl.pallas_call(
        functools.partial(finish_kernel, float(row_count * row_parts)),
        out_shape=(
            jax.ShapeDtypeStruct((own, 2 * nodes3, BINS), f32),
            jax.ShapeDtypeStruct((own, 2 * nodes4, BINS), f32),
            jax.ShapeDtypeStruct((1, leaves), f32),
            jax.ShapeDtypeStruct(square, f32),
            jax.ShapeDtypeStruct(square, f32),
        ),
        in_specs=[whole()] * 5,
        out_specs=(whole(),) * 5,
        scratch_shapes=[pltpu.VMEM((own * 2 * tags, LANES), f32)],
        compiler_params=pltpu.CompilerParams(vmem_limit_bytes=24 * 1024 * 1024),
    )(hist, path, label_sq, weight_sq, score_sq)
    return (
        hist3,
        hist4,
        values.reshape(leaves),
        new_scores.reshape(row_count),
        new_weights.reshape(row_count),
    )


def solution(mesh):
    placed = (P(None, "rows"), P("rows"), P("rows"), P("rows"), P("rows"), P(), P(), P(), P())
    return jax.shard_map(
        functools.partial(on_device, mesh.shape["rows"], mesh.shape["feat"]),
        mesh=mesh,
        in_specs=placed,
        out_specs=(P("feat", None, None), P("feat", None, None), P(), P("rows"), P("rows")),
        check_vma=False,
    )
```

```python
import functools

import jax
import jax.numpy as jnp
from jax import lax
from jax.experimental import pallas as pl
from jax.experimental.pallas import tpu as pltpu
from jax.sharding import PartitionSpec as P

BINS = 256
LANES = 128
SUB = 8
NT = (((1,), (1,)), ((), ()))


def grow_kernel(
    f3_hbm,
    b3_hbm,
    f4_hbm,
    b4_hbm,
    codes_hbm,
    node_hbm,
    label_hbm,
    weight_hbm,
    hist_ref,
    path_ref,
    f3_ref,
    b3_ref,
    f4_ref,
    b4_ref,
    codes_ref,
    node_ref,
    label_ref,
    weight_ref,
    low_ref,
    slot_ref,
    high_ref,
    sums_ref,
    leaf_ref,
    sems,
):
    groups = node_ref.shape[0]
    steps = groups // SUB
    own = low_ref.shape[0]
    nodes3 = f3_ref.shape[0]
    nodes4 = f4_ref.shape[0]
    tag_count = 2 * nodes4
    paths = 4 * nodes4
    moves = [
        pltpu.make_async_copy(source, target, sems.at[i])
        for i, (source, target) in enumerate(
            (
                (codes_hbm, codes_ref),
                (node_hbm, node_ref),
                (f3_hbm, f3_ref),
                (b3_hbm, b3_ref),
                (f4_hbm, f4_ref),
                (b4_hbm, b4_ref),
                (label_hbm, label_ref),
                (weight_hbm, weight_ref),
            )
        )
    ]
    for move in moves:
        move.start()
    sums_ref[...] = jnp.zeros_like(sums_ref)
    leaf_ref[...] = jnp.zeros_like(leaf_ref)
    for move in moves:
        move.wait()

    def code_start(feature):
        return (feature // SUB) * (groups * SUB) + feature % SUB

    def code_block(start, step):
        return codes_ref[pl.ds(start + step * (SUB * SUB), SUB, stride=SUB), :]

    def goes_right(nodes, feature_ref, bin_ref):
        margin = [jnp.zeros((SUB, LANES), jnp.int32) for _ in nodes]
        for n in range(feature_ref.shape[0]):
            start = code_start(feature_ref[n])
            cut = bin_ref[n]
            for step, node in enumerate(nodes):
                margin[step] = jnp.where(node == n, code_block(start, step) - cut, margin[step])
        return [jnp.where(m > 0, 1, 0) for m in margin]

    def rows_of(step):
        return slice(step * SUB, (step + 1) * SUB)

    node3 = [node_ref[rows_of(step), :] for step in range(steps)]
    right3 = goes_right(node3, f3_ref, b3_ref)
    node4 = [2 * n + r for n, r in zip(node3, right3)]
    right4 = goes_right(node4, f4_ref, b4_ref)
    first = lax.axis_index("feat") * own
    starts = [code_start(first + i) for i in range(own)]
    for step in range(steps):
        rows = rows_of(step)
        positive = jnp.where(label_ref[rows, :] > 0, 1, 0)
        tag = right3[step] * (2 * nodes3) + positive * nodes3 + node3[step]
        path_ref[rows, :] = positive * (2 * nodes4) + 2 * node4[step] + right4[step]
        for i in range(own):
            code = code_block(starts[i], step)
            low_ref[i, rows, :] = code & (LANES - 1)
            slot_ref[i, rows, :] = (code // LANES) * tag_count + tag
        high_ref[rows, :] = weight_ref[rows, :].astype(jnp.bfloat16).astype(jnp.float32)

    cell = (2 * SUB, LANES)
    iota = lax.broadcasted_iota(jnp.int32, cell, 0)
    small = jnp.int16
    ranks = [(iota + 2 * SUB * g).astype(small) for g in range(LANES // (2 * SUB))]
    one = jnp.ones(cell, jnp.bfloat16)
    nothing = jnp.zeros(cell, jnp.bfloat16)
    leaf_rank = [
        lax.broadcasted_iota(jnp.int32, (SUB, LANES), 0) + SUB * g for g in range(paths // SUB)
    ]

    def spread(ref, row, dtype, *lead):
        line = ref[(*lead, pl.ds(row, 1), slice(None))]
        return jnp.broadcast_to(line, cell).astype(dtype)

    def wide(ref, row):
        return jnp.broadcast_to(ref[pl.ds(row, 1), :], (SUB, LANES))

    def onehot(value, count, filled):
        parts = [jnp.where(value == ranks[g], filled, nothing) for g in range(count // (2 * SUB))]
        return jnp.concatenate(parts, axis=0)

    span = next(n for n in (24, 16, 8) if groups % n == 0)

    def tally(turn, carry):
        base = turn * span
        lines = range(span)
        heavy = [spread(high_ref, base + k, jnp.bfloat16) for k in lines]
        for i in range(own):
            slots = jnp.concatenate(
                [
                    onehot(spread(slot_ref, base + k, small, i), 2 * tag_count, heavy[k])
                    for k in lines
                ],
                axis=1,
            )
            lows = jnp.concatenate(
                [onehot(spread(low_ref, base + k, small, i), LANES, one) for k in lines],
                axis=1,
            )
            sums_ref[i] += lax.dot_general(lows, slots, NT, preferred_element_type=jnp.float32)
        count = paths // SUB
        exact = [leaf_ref[0, rows_of(g), :] for g in range(count)]
        rounded = [leaf_ref[1, rows_of(g), :] for g in range(count)]
        for k in lines:
            path = wide(path_ref, base + k)
            weight = wide(weight_ref, base + k)
            high = wide(high_ref, base + k)
            for g in range(count):
                here = path == leaf_rank[g]
                exact[g] += jnp.where(here, weight, 0.0)
                rounded[g] += jnp.where(here, high, 0.0)
        for g in range(count):
            leaf_ref[0, rows_of(g), :] = exact[g]
            leaf_ref[1, rows_of(g), :] = rounded[g]
        return carry

    lax.fori_loop(0, groups // span, tally, 0)
    for i in range(own // 2):
        hist_ref[i * LANES : (i + 1) * LANES, :] = jnp.concatenate(
            [sums_ref[2 * i], sums_ref[2 * i + 1]], axis=1
        )
    spot = lax.broadcasted_iota(jnp.int32, (paths, LANES), 0)
    lane = lax.broadcasted_iota(jnp.int32, (paths, LANES), 1)
    lines = []
    for kind in range(2):
        column = jnp.sum(leaf_ref[kind], axis=1, keepdims=True)
        lines.append(
            jnp.sum(jnp.where(spot == lane, column, 0.0), axis=0, keepdims=True)
        )
    tail = jnp.concatenate(lines + [jnp.zeros((SUB - 2, LANES), jnp.float32)], axis=0)
    hist_ref[own // 2 * LANES : own // 2 * LANES + SUB, :] = tail


def finish_kernel(
    total,
    hist_ref,
    path_ref,
    weight_ref,
    score_ref,
    hist3_ref,
    hist4_ref,
    value_ref,
    new_score_ref,
    new_weight_ref,
    weave_ref,
):
    own, tags, _ = hist4_ref.shape
    nodes4 = tags // 2
    nodes3 = nodes4 // 2
    leaves = value_ref.shape[1]
    for pair in range(own // 2):
        turned = hist_ref[pair * LANES : (pair + 1) * LANES, :].T
        for q in range(4):
            i = 2 * pair + q // 2
            h = q % 2
            lanes = slice(h * LANES, (h + 1) * LANES)
            start = q * tags
            keep = (pair * 4 + q) * tags

            def tag_rows(right, positive):
                first = start + right * 2 * nodes3 + positive * nodes3
                return turned[first : first + nodes3, :]

            sums = [tag_rows(r, 1) + tag_rows(r, 0) for r in range(2)]
            diffs = [tag_rows(r, 1) - tag_rows(r, 0) for r in range(2)]
            hist3_ref[i, 0:nodes3, lanes] = sums[0] + sums[1]
            hist3_ref[i, nodes3 : 2 * nodes3, lanes] = diffs[0] + diffs[1]
            for r in range(2):
                weave_ref[pl.ds(keep + r, nodes3, stride=2), :] = sums[r]
                weave_ref[pl.ds(keep + nodes4 + r, nodes3, stride=2), :] = diffs[r]
            hist4_ref[i, :, lanes] = weave_ref[keep : keep + tags, :]
    leaf_base = own // 2 * LANES
    pieces = hist_ref[leaf_base : leaf_base + SUB, :]
    lane = lax.broadcasted_iota(jnp.int32, (1, LANES), 1)
    full = pieces[0:1, :]
    rounded = pieces[1:2, :]
    other = pltpu.roll(rounded, LANES - leaves, 1)
    values = (other - rounded) / (other + rounded + 1.0)
    value_ref[...] = values[:, 0:leaves]
    negative = lane < leaves
    both = jnp.where(negative, values, pltpu.roll(values, leaves, 1))
    both = jnp.where(lane < 2 * leaves, both, 0.0)
    growth = jnp.exp(jnp.where(negative, both, -both))
    grand = jnp.sum(full * growth, axis=1, keepdims=True)
    factor = growth * (total / grand)
    factor8 = jnp.broadcast_to(factor, (SUB, LANES))
    both8 = jnp.broadcast_to(both, (SUB, LANES))
    for step in range(path_ref.shape[0] // SUB):
        rows = slice(step * SUB, (step + 1) * SUB)
        path = path_ref[rows, :]
        scale = jnp.take_along_axis(factor8, path, axis=1)
        shift = jnp.take_along_axis(both8, path, axis=1)
        new_weight_ref[rows, :] = weight_ref[rows, :] * scale
        new_score_ref[rows, :] = score_ref[rows, :] + shift


def combine_rows(part, axis, size):
    if size & (size - 1):
        return lax.psum(part, axis)
    reach = 1
    while reach < size:
        pairs = [(i, i ^ reach) for i in range(size)]
        part = part + lax.ppermute(part, axis, pairs)
        reach *= 2
    return part


def whole(memory=pltpu.VMEM):
    return pl.BlockSpec(memory_space=memory)


def on_device(
    row_parts,
    feat_parts,
    bin_codes,
    node_ids,
    labels,
    weights,
    predictions,
    level3_feature,
    level3_bin,
    level4_feature,
    level4_bin,
):
    features, row_count = bin_codes.shape
    groups = row_count // LANES
    own = features // feat_parts
    nodes3 = level3_feature.shape[0]
    nodes4 = level4_feature.shape[0]
    leaves = 2 * nodes4
    tags = 2 * nodes4
    codes = (
        bin_codes.reshape(features // SUB, SUB, groups, LANES)
        .transpose(0, 2, 1, 3)
        .reshape(features * groups, LANES)
    )
    square = (groups, LANES)
    node_sq = node_ids.reshape(square)
    label_sq = labels.reshape(square)
    weight_sq = weights.reshape(square)
    score_sq = predictions.reshape(square)
    hist_rows = own // 2 * LANES + SUB
    f32, i32 = jnp.float32, jnp.int32
    held = functools.partial(pltpu.with_memory_space_constraint, memory_space=pltpu.HBM)
    hist, path = pl.pallas_call(
        grow_kernel,
        out_shape=(pltpu.VMEM((hist_rows, LANES), f32), pltpu.VMEM(square, i32)),
        in_specs=[whole(pltpu.HBM)] * 8,
        out_specs=(whole(), whole()),
        scratch_shapes=[
            pltpu.SMEM((nodes3,), i32),
            pltpu.SMEM((nodes3,), i32),
            pltpu.SMEM((nodes4,), i32),
            pltpu.SMEM((nodes4,), i32),
            pltpu.VMEM(codes.shape, i32),
            pltpu.VMEM(square, i32),
            pltpu.VMEM(square, f32),
            pltpu.VMEM(square, f32),
            pltpu.VMEM((own, *square), i32),
            pltpu.VMEM((own, *square), i32),
            pltpu.VMEM(square, f32),
            pltpu.VMEM((own, LANES, 2 * tags), f32),
            pltpu.VMEM((2, 2 * leaves, LANES), f32),
            pltpu.SemaphoreType.DMA((8,)),
        ],
        compiler_params=pltpu.CompilerParams(vmem_limit_bytes=24 * 1024 * 1024),
    )(
        held(level3_feature),
        held(level3_bin),
        held(level4_feature),
        held(level4_bin),
        held(codes),
        held(node_sq),
        held(label_sq),
        held(weight_sq),
    )
    hist = combine_rows(hist, "rows", row_parts)
    hist3, hist4, values, new_scores, new_weights = pl.pallas_call(
        functools.partial(finish_kernel, float(row_count * row_parts)),
        out_shape=(
            jax.ShapeDtypeStruct((own, 2 * nodes3, BINS), f32),
            jax.ShapeDtypeStruct((own, 2 * nodes4, BINS), f32),
            jax.ShapeDtypeStruct((1, leaves), f32),
            jax.ShapeDtypeStruct(square, f32),
            jax.ShapeDtypeStruct(square, f32),
        ),
        in_specs=[whole()] * 4,
        out_specs=(whole(),) * 5,
        scratch_shapes=[pltpu.VMEM((own * 2 * tags, LANES), f32)],
        compiler_params=pltpu.CompilerParams(vmem_limit_bytes=24 * 1024 * 1024),
    )(hist, path, weight_sq, score_sq)
    return (
        hist3,
        hist4,
        values.reshape(leaves),
        new_scores.reshape(row_count),
        new_weights.reshape(row_count),
    )


def solution(mesh):
    placed = (P(None, "rows"), P("rows"), P("rows"), P("rows"), P("rows"), P(), P(), P(), P())
    return jax.shard_map(
        functools.partial(on_device, mesh.shape["rows"], mesh.shape["feat"]),
        mesh=mesh,
        in_specs=placed,
        out_specs=(P("feat", None, None), P("feat", None, None), P(), P("rows"), P("rows")),
        check_vma=False,
    )
```

```python
import functools

import jax
import jax.numpy as jnp
from jax import lax
from jax.experimental import pallas as pl
from jax.experimental.pallas import tpu as pltpu
from jax.sharding import PartitionSpec as P

BINS = 256
LANES = 128
SUB = 8
NT = (((1,), (1,)), ((), ()))


def grow_kernel(
    f3_hbm,
    b3_hbm,
    f4_hbm,
    b4_hbm,
    codes_hbm,
    node_hbm,
    label_hbm,
    weight_hbm,
    hist_ref,
    path_ref,
    f3_ref,
    b3_ref,
    f4_ref,
    b4_ref,
    codes_ref,
    node_ref,
    label_ref,
    weight_ref,
    low_ref,
    slot_ref,
    high_ref,
    sums_ref,
    leaf_ref,
    sems,
):
    groups = node_ref.shape[0]
    steps = groups // SUB
    own = low_ref.shape[0]
    nodes3 = f3_ref.shape[0]
    nodes4 = f4_ref.shape[0]
    tag_count = 2 * nodes4
    paths = 4 * nodes4
    moves = [
        pltpu.make_async_copy(source, target, sems.at[i])
        for i, (source, target) in enumerate(
            (
                (codes_hbm, codes_ref),
                (node_hbm, node_ref),
                (f3_hbm, f3_ref),
                (b3_hbm, b3_ref),
                (f4_hbm, f4_ref),
                (b4_hbm, b4_ref),
                (label_hbm, label_ref),
                (weight_hbm, weight_ref),
            )
        )
    ]
    for move in moves:
        move.start()
    sums_ref[...] = jnp.zeros_like(sums_ref)
    leaf_ref[...] = jnp.zeros_like(leaf_ref)
    for move in moves:
        move.wait()

    def code_start(feature):
        return (feature // SUB) * (groups * SUB) + feature % SUB

    def code_block(start, step):
        return codes_ref[pl.ds(start + step * (SUB * SUB), SUB, stride=SUB), :]

    def goes_right(nodes, feature_ref, bin_ref):
        margin = [jnp.zeros((SUB, LANES), jnp.int32) for _ in nodes]
        for n in range(feature_ref.shape[0]):
            start = code_start(feature_ref[n])
            cut = bin_ref[n]
            for step, node in enumerate(nodes):
                margin[step] = jnp.where(node == n, code_block(start, step) - cut, margin[step])
        return [jnp.where(m > 0, 1, 0) for m in margin]

    def rows_of(step):
        return slice(step * SUB, (step + 1) * SUB)

    node3 = [node_ref[rows_of(step), :] for step in range(steps)]
    right3 = goes_right(node3, f3_ref, b3_ref)
    node4 = [2 * n + r for n, r in zip(node3, right3)]
    right4 = goes_right(node4, f4_ref, b4_ref)
    first = lax.axis_index("feat") * own
    starts = [code_start(first + i) for i in range(own)]
    for step in range(steps):
        rows = rows_of(step)
        positive = jnp.where(label_ref[rows, :] > 0, 1, 0)
        tag = right3[step] * (2 * nodes3) + positive * nodes3 + node3[step]
        path_ref[rows, :] = positive * (2 * nodes4) + 2 * node4[step] + right4[step]
        for i in range(own):
            code = code_block(starts[i], step)
            low_ref[i, rows, :] = code & (LANES - 1)
            slot_ref[i, rows, :] = (code // LANES) * tag_count + tag
        high_ref[rows, :] = weight_ref[rows, :].astype(jnp.bfloat16).astype(jnp.float32)

    cell = (2 * SUB, LANES)
    iota = lax.broadcasted_iota(jnp.int32, cell, 0)
    small = jnp.int16
    ranks = [(iota + 2 * SUB * g).astype(small) for g in range(LANES // (2 * SUB))]
    one = jnp.ones(cell, jnp.bfloat16)
    nothing = jnp.zeros(cell, jnp.bfloat16)
    leaf_rank = [
        lax.broadcasted_iota(jnp.int32, (SUB, LANES), 0) + SUB * g for g in range(paths // SUB)
    ]

    def spread(ref, row, dtype, *lead):
        line = ref[(*lead, pl.ds(row, 1), slice(None))]
        return jnp.broadcast_to(line, cell).astype(dtype)

    def wide(ref, row):
        return jnp.broadcast_to(ref[pl.ds(row, 1), :], (SUB, LANES))

    def onehot(value, count, filled):
        parts = [jnp.where(value == ranks[g], filled, nothing) for g in range(count // (2 * SUB))]
        return jnp.concatenate(parts, axis=0)

    span = next(n for n in (120, 24, 16, 8) if groups % n == 0)

    def tally(turn, carry):
        base = turn * span
        lines = range(span)
        heavy = [spread(high_ref, base + k, jnp.bfloat16) for k in lines]
        for i in range(own):
            slots = jnp.concatenate(
                [
                    onehot(spread(slot_ref, base + k, small, i), 2 * tag_count, heavy[k])
                    for k in lines
                ],
                axis=1,
            )
            lows = jnp.concatenate(
                [onehot(spread(low_ref, base + k, small, i), LANES, one) for k in lines],
                axis=1,
            )
            sums_ref[i] += lax.dot_general(lows, slots, NT, preferred_element_type=jnp.float32)
        count = paths // SUB
        exact = [leaf_ref[0, rows_of(g), :] for g in range(count)]
        rounded = [leaf_ref[1, rows_of(g), :] for g in range(count)]
        for k in lines:
            path = wide(path_ref, base + k)
            weight = wide(weight_ref, base + k)
            high = wide(high_ref, base + k)
            for g in range(count):
                here = path == leaf_rank[g]
                exact[g] += jnp.where(here, weight, 0.0)
                rounded[g] += jnp.where(here, high, 0.0)
        for g in range(count):
            leaf_ref[0, rows_of(g), :] = exact[g]
            leaf_ref[1, rows_of(g), :] = rounded[g]
        return carry

    lax.fori_loop(0, groups // span, tally, 0)
    for i in range(own // 2):
        hist_ref[i * LANES : (i + 1) * LANES, :] = jnp.concatenate(
            [sums_ref[2 * i], sums_ref[2 * i + 1]], axis=1
        )
    spot = lax.broadcasted_iota(jnp.int32, (paths, LANES), 0)
    lane = lax.broadcasted_iota(jnp.int32, (paths, LANES), 1)
    lines = []
    for kind in range(2):
        column = jnp.sum(leaf_ref[kind], axis=1, keepdims=True)
        lines.append(
            jnp.sum(jnp.where(spot == lane, column, 0.0), axis=0, keepdims=True)
        )
    tail = jnp.concatenate(lines + [jnp.zeros((SUB - 2, LANES), jnp.float32)], axis=0)
    hist_ref[own // 2 * LANES : own // 2 * LANES + SUB, :] = tail


def finish_kernel(
    total,
    hist_ref,
    path_ref,
    weight_ref,
    score_ref,
    hist3_ref,
    hist4_ref,
    value_ref,
    new_score_ref,
    new_weight_ref,
    weave_ref,
):
    own, tags, _ = hist4_ref.shape
    nodes4 = tags // 2
    nodes3 = nodes4 // 2
    leaves = value_ref.shape[1]
    for pair in range(own // 2):
        turned = hist_ref[pair * LANES : (pair + 1) * LANES, :].T
        for q in range(4):
            i = 2 * pair + q // 2
            h = q % 2
            lanes = slice(h * LANES, (h + 1) * LANES)
            start = q * tags
            keep = (pair * 4 + q) * tags

            def tag_rows(right, positive):
                first = start + right * 2 * nodes3 + positive * nodes3
                return turned[first : first + nodes3, :]

            sums = [tag_rows(r, 1) + tag_rows(r, 0) for r in range(2)]
            diffs = [tag_rows(r, 1) - tag_rows(r, 0) for r in range(2)]
            hist3_ref[i, 0:nodes3, lanes] = sums[0] + sums[1]
            hist3_ref[i, nodes3 : 2 * nodes3, lanes] = diffs[0] + diffs[1]
            for r in range(2):
                weave_ref[pl.ds(keep + r, nodes3, stride=2), :] = sums[r]
                weave_ref[pl.ds(keep + nodes4 + r, nodes3, stride=2), :] = diffs[r]
            hist4_ref[i, :, lanes] = weave_ref[keep : keep + tags, :]
    leaf_base = own // 2 * LANES
    pieces = hist_ref[leaf_base : leaf_base + SUB, :]
    lane = lax.broadcasted_iota(jnp.int32, (1, LANES), 1)
    full = pieces[0:1, :]
    rounded = pieces[1:2, :]
    other = pltpu.roll(rounded, LANES - leaves, 1)
    values = (other - rounded) / (other + rounded + 1.0)
    value_ref[...] = values[:, 0:leaves]
    negative = lane < leaves
    both = jnp.where(negative, values, pltpu.roll(values, leaves, 1))
    both = jnp.where(lane < 2 * leaves, both, 0.0)
    growth = jnp.exp(jnp.where(negative, both, -both))
    grand = jnp.sum(full * growth, axis=1, keepdims=True)
    factor = growth * (total / grand)
    factor8 = jnp.broadcast_to(factor, (SUB, LANES))
    both8 = jnp.broadcast_to(both, (SUB, LANES))
    for step in range(path_ref.shape[0] // SUB):
        rows = slice(step * SUB, (step + 1) * SUB)
        path = path_ref[rows, :]
        scale = jnp.take_along_axis(factor8, path, axis=1)
        shift = jnp.take_along_axis(both8, path, axis=1)
        new_weight_ref[rows, :] = weight_ref[rows, :] * scale
        new_score_ref[rows, :] = score_ref[rows, :] + shift


def combine_rows(part, row_parts, feat_parts):
    if row_parts & (row_parts - 1):
        return lax.psum(part, "rows")
    bits = row_parts.bit_length() - 1
    for step in range(bits):
        pairs = []
        for row in range(row_parts):
            for feat in range(feat_parts):
                other = row ^ reach(feat, step, bits)
                pairs.append((row * feat_parts + feat, other * feat_parts + feat))
        part = part + lax.ppermute(part, ("rows", "feat"), pairs)
    return part


def reach(feat, step, bits):
    return 1 << (step + feat % 2 * (bits - 1)) % bits


def whole(memory=pltpu.VMEM):
    return pl.BlockSpec(memory_space=memory)


def on_device(
    row_parts,
    feat_parts,
    bin_codes,
    node_ids,
    labels,
    weights,
    predictions,
    level3_feature,
    level3_bin,
    level4_feature,
    level4_bin,
):
    features, row_count = bin_codes.shape
    groups = row_count // LANES
    own = features // feat_parts
    nodes3 = level3_feature.shape[0]
    nodes4 = level4_feature.shape[0]
    leaves = 2 * nodes4
    tags = 2 * nodes4
    codes = (
        bin_codes.reshape(features // SUB, SUB, groups, LANES)
        .transpose(0, 2, 1, 3)
        .reshape(features * groups, LANES)
    )
    square = (groups, LANES)
    node_sq = node_ids.reshape(square)
    label_sq = labels.reshape(square)
    weight_sq = weights.reshape(square)
    score_sq = predictions.reshape(square)
    hist_rows = own // 2 * LANES + SUB
    f32, i32 = jnp.float32, jnp.int32
    held = functools.partial(pltpu.with_memory_space_constraint, memory_space=pltpu.HBM)
    hist, path = pl.pallas_call(
        grow_kernel,
        out_shape=(pltpu.VMEM((hist_rows, LANES), f32), pltpu.VMEM(square, i32)),
        in_specs=[whole(pltpu.HBM)] * 8,
        out_specs=(whole(), whole()),
        scratch_shapes=[
            pltpu.SMEM((nodes3,), i32),
            pltpu.SMEM((nodes3,), i32),
            pltpu.SMEM((nodes4,), i32),
            pltpu.SMEM((nodes4,), i32),
            pltpu.VMEM(codes.shape, i32),
            pltpu.VMEM(square, i32),
            pltpu.VMEM(square, f32),
            pltpu.VMEM(square, f32),
            pltpu.VMEM((own, *square), i32),
            pltpu.VMEM((own, *square), i32),
            pltpu.VMEM(square, f32),
            pltpu.VMEM((own, LANES, 2 * tags), f32),
            pltpu.VMEM((2, 2 * leaves, LANES), f32),
            pltpu.SemaphoreType.DMA((8,)),
        ],
        compiler_params=pltpu.CompilerParams(vmem_limit_bytes=24 * 1024 * 1024),
    )(
        held(level3_feature),
        held(level3_bin),
        held(level4_feature),
        held(level4_bin),
        held(codes),
        held(node_sq),
        held(label_sq),
        held(weight_sq),
    )
    hist = combine_rows(hist, row_parts, feat_parts)
    hist3, hist4, values, new_scores, new_weights = pl.pallas_call(
        functools.partial(finish_kernel, float(row_count * row_parts)),
        out_shape=(
            jax.ShapeDtypeStruct((own, 2 * nodes3, BINS), f32),
            jax.ShapeDtypeStruct((own, 2 * nodes4, BINS), f32),
            jax.ShapeDtypeStruct((1, leaves), f32),
            jax.ShapeDtypeStruct(square, f32),
            jax.ShapeDtypeStruct(square, f32),
        ),
        in_specs=[whole()] * 4,
        out_specs=(whole(),) * 5,
        scratch_shapes=[pltpu.VMEM((own * 2 * tags, LANES), f32)],
        compiler_params=pltpu.CompilerParams(vmem_limit_bytes=24 * 1024 * 1024),
    )(hist, path, weight_sq, score_sq)
    return (
        hist3,
        hist4,
        values.reshape(leaves),
        new_scores.reshape(row_count),
        new_weights.reshape(row_count),
    )


def solution(mesh):
    placed = (P(None, "rows"), P("rows"), P("rows"), P("rows"), P("rows"), P(), P(), P(), P())
    return jax.shard_map(
        functools.partial(on_device, mesh.shape["rows"], mesh.shape["feat"]),
        mesh=mesh,
        in_specs=placed,
        out_specs=(P("feat", None, None), P("feat", None, None), P(), P("rows"), P("rows")),
        check_vma=False,
    )
```

```python
import functools

import jax
import jax.numpy as jnp
from jax import lax
from jax.experimental import pallas as pl
from jax.experimental.pallas import tpu as pltpu
from jax.sharding import PartitionSpec as P

BINS = 256
LANES = 128
SUB = 8
DEPTH = 256
NT = (((1,), (1,)), ((), ()))


def grow_kernel(
    f3_hbm,
    b3_hbm,
    f4_hbm,
    b4_hbm,
    codes_hbm,
    node_hbm,
    label_hbm,
    weight_hbm,
    hist_ref,
    path_ref,
    f3_ref,
    b3_ref,
    f4_ref,
    b4_ref,
    codes_ref,
    node_ref,
    label_ref,
    weight_ref,
    low_ref,
    slot_ref,
    high_ref,
    piece_ref,
    sems,
):
    groups = node_ref.shape[0]
    steps = groups // SUB
    own = low_ref.shape[0]
    nodes3 = f3_ref.shape[0]
    nodes4 = f4_ref.shape[0]
    tag_count = 2 * nodes4
    moves = [
        pltpu.make_async_copy(source, target, sems.at[i])
        for i, (source, target) in enumerate(
            (
                (codes_hbm, codes_ref),
                (node_hbm, node_ref),
                (f3_hbm, f3_ref),
                (b3_hbm, b3_ref),
                (f4_hbm, f4_ref),
                (b4_hbm, b4_ref),
                (label_hbm, label_ref),
                (weight_hbm, weight_ref),
            )
        )
    ]
    for move in moves:
        move.start()
    piece_ref[...] = jnp.zeros_like(piece_ref)
    for move in moves:
        move.wait()

    def code_start(feature):
        return (feature // SUB) * (groups * SUB) + feature % SUB

    def code_block(start, step):
        return codes_ref[pl.ds(start + step * (SUB * SUB), SUB, stride=SUB), :]

    def goes_right(nodes, feature_ref, bin_ref):
        margin = [jnp.zeros((SUB, LANES), jnp.int32) for _ in nodes]
        for n in range(feature_ref.shape[0]):
            start = code_start(feature_ref[n])
            cut = bin_ref[n]
            for step, node in enumerate(nodes):
                margin[step] = jnp.where(node == n, code_block(start, step) - cut, margin[step])
        return [jnp.where(m > 0, 1, 0) for m in margin]

    def rows_of(step):
        return slice(step * SUB, (step + 1) * SUB)

    node3 = [node_ref[rows_of(step), :] for step in range(steps)]
    right3 = goes_right(node3, f3_ref, b3_ref)
    node4 = [2 * n + r for n, r in zip(node3, right3)]
    right4 = goes_right(node4, f4_ref, b4_ref)
    first = lax.axis_index("feat") * own
    starts = [code_start(first + i) for i in range(own)]
    for step in range(steps):
        rows = rows_of(step)
        positive = jnp.where(label_ref[rows, :] > 0, 1, 0)
        tag = right3[step] * (2 * nodes3) + positive * nodes3 + node3[step]
        path_ref[rows, :] = right4[step] * tag_count + tag
        for i in range(own):
            code = code_block(starts[i], step)
            low_ref[i, rows, :] = code & (LANES - 1)
            slot_ref[i, rows, :] = (code // LANES) * tag_count + tag
        weight = weight_ref[rows, :]
        high = weight.astype(jnp.bfloat16).astype(jnp.float32)
        mid = (weight - high).astype(jnp.bfloat16).astype(jnp.float32)
        high_ref[rows, :] = high
        for k, piece in enumerate((high, mid, weight - high - mid)):
            for side in range(2):
                spots = pl.ds(step * (SUB * SUB) + 2 * k + side, SUB, stride=SUB)
                piece_ref[spots, :] = jnp.where(right4[step] == side, piece, 0.0)

    cell = (2 * SUB, LANES)
    iota = lax.broadcasted_iota(jnp.int32, cell, 0)
    small = jnp.int16
    ranks = [(iota + 2 * SUB * g).astype(small) for g in range(LANES // (2 * SUB))]
    one = jnp.ones(cell, jnp.bfloat16)
    nothing = jnp.zeros(cell, jnp.bfloat16)
    def spread(ref, row, dtype, *lead):
        line = ref[(*lead, pl.ds(row, 1), slice(None))]
        return jnp.broadcast_to(line, cell).astype(dtype)

    def onehot(value, count, filled):
        parts = [jnp.where(value == ranks[g], filled, nothing) for g in range(count // (2 * SUB))]
        return jnp.concatenate(parts, axis=0)

    halves = DEPTH // LANES
    tiles = groups // halves
    units = 2

    def fill(tile):
        lines = range(tile * halves, (tile + 1) * halves)
        columns = [
            jnp.concatenate(
                [
                    onehot(spread(slot_ref, line, small, i), 2 * tag_count, one)
                    for i in range(own)
                ],
                axis=0,
            )
            for line in lines
        ]
        pltpu.matmul_push_rhs(
            jnp.concatenate(columns, axis=1), tile // units % 2, tile % units, transpose=True
        )

    def stream(tile, accs):
        columns = []
        for line in range(tile * halves, (tile + 1) * halves):
            heavy = spread(high_ref, line, jnp.bfloat16)
            parts = [onehot(spread(low_ref, line, small, i), LANES, heavy) for i in range(own)]
            pieces = piece_ref[line * SUB : (line + 1) * SUB, :]
            parts.append(
                jnp.concatenate([pieces, jnp.zeros_like(pieces)], axis=0).astype(jnp.bfloat16)
            )
            columns.append(jnp.concatenate(parts, axis=0))
        pltpu.matmul_acc_lhs(
            accs[tile % units], jnp.concatenate(columns, axis=1), tile // units % 2
        )

    def product(*accs):
        for tile in range(units):
            fill(tile)
        for tile in range(tiles):
            if tile + units < tiles:
                fill(tile + units)
            stream(tile, accs)
        return pltpu.matmul_pop(accs[0]) + pltpu.matmul_pop(accs[1])

    shape = (own * LANES + 2 * SUB, DEPTH)
    sums = pl.run_scoped(
        product, *(pltpu.ACC(unit)(shape, jnp.float32) for unit in range(units))
    )
    left = lax.broadcasted_iota(jnp.int32, (LANES, LANES), 1) < 2 * tag_count
    for pair in range(own // 2):
        lanes = slice(pair * LANES, (pair + 1) * LANES)
        rows = [slice(i * LANES, (i + 1) * LANES) for i in (2 * pair, 2 * pair + 1)]
        hist_ref[lanes, :] = jnp.where(left, sums[rows[0], lanes], sums[rows[1], lanes])
    doubled = sums[own * LANES : own * LANES + SUB, 0:LANES]
    hist_ref[own // 2 * LANES : own // 2 * LANES + SUB, :] = doubled + pltpu.roll(
        doubled, LANES - tag_count, 1
    )


def finish_kernel(
    total,
    hist_ref,
    path_ref,
    weight_ref,
    score_ref,
    hist3_ref,
    hist4_ref,
    value_ref,
    new_score_ref,
    new_weight_ref,
    weave_ref,
):
    own, tags, _ = hist4_ref.shape
    nodes4 = tags // 2
    nodes3 = nodes4 // 2
    leaves = value_ref.shape[1]
    for pair in range(own // 2):
        turned = hist_ref[pair * LANES : (pair + 1) * LANES, :].T
        for q in range(4):
            i = 2 * pair + q // 2
            h = q % 2
            lanes = slice(h * LANES, (h + 1) * LANES)
            start = q * tags
            keep = (pair * 4 + q) * tags

            def tag_rows(right, positive):
                first = start + right * 2 * nodes3 + positive * nodes3
                return turned[first : first + nodes3, :]

            sums = [tag_rows(r, 1) + tag_rows(r, 0) for r in range(2)]
            diffs = [tag_rows(r, 1) - tag_rows(r, 0) for r in range(2)]
            hist3_ref[i, 0:nodes3, lanes] = sums[0] + sums[1]
            hist3_ref[i, nodes3 : 2 * nodes3, lanes] = diffs[0] + diffs[1]
            for r in range(2):
                weave_ref[pl.ds(keep + r, nodes3, stride=2), :] = sums[r]
                weave_ref[pl.ds(keep + nodes4 + r, nodes3, stride=2), :] = diffs[r]
            hist4_ref[i, :, lanes] = weave_ref[keep : keep + tags, :]
    leaf_base = own // 2 * LANES
    pieces = hist_ref[leaf_base : leaf_base + SUB, :]
    lane = lax.broadcasted_iota(jnp.int32, (1, LANES), 1)
    right = (lane & tags) > 0
    positive = (lane & nodes3) > 0

    def both_sides(k):
        return jnp.where(
            right, pltpu.roll(pieces[2 * k + 1 : 2 * k + 2, :], tags, 1), pieces[2 * k : 2 * k + 1, :]
        )

    def partner(line):
        return jnp.where(
            positive, pltpu.roll(line, nodes3, 1), pltpu.roll(line, LANES - nodes3, 1)
        )

    rounded = both_sides(0)
    full = rounded + (both_sides(1) + both_sides(2))
    inside = lane < 2 * tags
    other = partner(rounded)
    gap = jnp.where(positive, rounded - other, other - rounded)
    values = jnp.where(inside, gap / (rounded + other + 1.0), 0.0)
    growth = jnp.exp(jnp.where(positive, -values, values))
    grand = jnp.sum(jnp.where(inside, full * growth, 0.0), axis=1, keepdims=True)
    factor = growth * (total / grand)
    factor8 = jnp.broadcast_to(factor, (SUB, LANES))
    both8 = jnp.broadcast_to(values, (SUB, LANES))
    leaf = lax.broadcasted_iota(jnp.int32, (SUB, LANES), 1)
    spot = (leaf & 1) * tags + ((leaf >> 1) & 1) * (2 * nodes3) + ((leaf >> 2) & (nodes3 - 1))
    value_ref[...] = jnp.take_along_axis(both8, spot, axis=1)[0:1, 0:leaves]
    for step in range(path_ref.shape[0] // SUB):
        rows = slice(step * SUB, (step + 1) * SUB)
        path = path_ref[rows, :]
        scale = jnp.take_along_axis(factor8, path, axis=1)
        shift = jnp.take_along_axis(both8, path, axis=1)
        new_weight_ref[rows, :] = weight_ref[rows, :] * scale
        new_score_ref[rows, :] = score_ref[rows, :] + shift


def combine_rows(part, row_parts, feat_parts):
    if row_parts & (row_parts - 1):
        return lax.psum(part, "rows")
    bits = row_parts.bit_length() - 1
    for step in range(bits):
        pairs = []
        for row in range(row_parts):
            for feat in range(feat_parts):
                other = row ^ reach(feat, step, bits)
                pairs.append((row * feat_parts + feat, other * feat_parts + feat))
        part = part + lax.ppermute(part, ("rows", "feat"), pairs)
    return part


def reach(feat, step, bits):
    return 1 << (step + feat % 2 * (bits - 1)) % bits


def whole(memory=pltpu.VMEM):
    return pl.BlockSpec(memory_space=memory)


def on_device(
    row_parts,
    feat_parts,
    bin_codes,
    node_ids,
    labels,
    weights,
    predictions,
    level3_feature,
    level3_bin,
    level4_feature,
    level4_bin,
):
    features, row_count = bin_codes.shape
    groups = row_count // LANES
    own = features // feat_parts
    nodes3 = level3_feature.shape[0]
    nodes4 = level4_feature.shape[0]
    leaves = 2 * nodes4
    tags = 2 * nodes4
    codes = (
        bin_codes.reshape(features // SUB, SUB, groups, LANES)
        .transpose(0, 2, 1, 3)
        .reshape(features * groups, LANES)
    )
    square = (groups, LANES)
    node_sq = node_ids.reshape(square)
    label_sq = labels.reshape(square)
    weight_sq = weights.reshape(square)
    score_sq = predictions.reshape(square)
    hist_rows = own // 2 * LANES + SUB
    f32, i32 = jnp.float32, jnp.int32
    held = functools.partial(pltpu.with_memory_space_constraint, memory_space=pltpu.HBM)
    hist, path = pl.pallas_call(
        grow_kernel,
        out_shape=(pltpu.VMEM((hist_rows, LANES), f32), pltpu.VMEM(square, i32)),
        in_specs=[whole(pltpu.HBM)] * 8,
        out_specs=(whole(), whole()),
        scratch_shapes=[
            pltpu.SMEM((nodes3,), i32),
            pltpu.SMEM((nodes3,), i32),
            pltpu.SMEM((nodes4,), i32),
            pltpu.SMEM((nodes4,), i32),
            pltpu.VMEM(codes.shape, i32),
            pltpu.VMEM(square, i32),
            pltpu.VMEM(square, f32),
            pltpu.VMEM(square, f32),
            pltpu.VMEM((own, *square), i32),
            pltpu.VMEM((own, *square), i32),
            pltpu.VMEM(square, f32),
            pltpu.VMEM((groups * SUB, LANES), f32),
            pltpu.SemaphoreType.DMA((8,)),
        ],
        compiler_params=pltpu.CompilerParams(vmem_limit_bytes=24 * 1024 * 1024),
    )(
        held(level3_feature),
        held(level3_bin),
        held(level4_feature),
        held(level4_bin),
        held(codes),
        held(node_sq),
        held(label_sq),
        held(weight_sq),
    )
    hist = combine_rows(hist, row_parts, feat_parts)
    hist3, hist4, values, new_scores, new_weights = pl.pallas_call(
        functools.partial(finish_kernel, float(row_count * row_parts)),
        out_shape=(
            jax.ShapeDtypeStruct((own, 2 * nodes3, BINS), f32),
            jax.ShapeDtypeStruct((own, 2 * nodes4, BINS), f32),
            jax.ShapeDtypeStruct((1, leaves), f32),
            jax.ShapeDtypeStruct(square, f32),
            jax.ShapeDtypeStruct(square, f32),
        ),
        in_specs=[whole()] * 4,
        out_specs=(whole(),) * 5,
        scratch_shapes=[pltpu.VMEM((own * 2 * tags, LANES), f32)],
        compiler_params=pltpu.CompilerParams(vmem_limit_bytes=24 * 1024 * 1024),
    )(hist, path, weight_sq, score_sq)
    return (
        hist3,
        hist4,
        values.reshape(leaves),
        new_scores.reshape(row_count),
        new_weights.reshape(row_count),
    )


def solution(mesh):
    placed = (P(None, "rows"), P("rows"), P("rows"), P("rows"), P("rows"), P(), P(), P(), P())
    return jax.shard_map(
        functools.partial(on_device, mesh.shape["rows"], mesh.shape["feat"]),
        mesh=mesh,
        in_specs=placed,
        out_specs=(P("feat", None, None), P("feat", None, None), P(), P("rows"), P("rows")),
        check_vma=False,
    )
```

```python
import functools

import jax
import jax.numpy as jnp
from jax import lax
from jax.experimental import pallas as pl
from jax.experimental.pallas import tpu as pltpu
from jax.sharding import PartitionSpec as P

BINS = 256
LANES = 128
SUB = 8
DEPTH = 256
NT = (((1,), (1,)), ((), ()))


def grow_kernel(
    f3_ref,
    b3_ref,
    f4_ref,
    b4_ref,
    codes_ref,
    node_ref,
    label_ref,
    weight_ref,
    hist_ref,
    path_ref,
    low_ref,
    slot_ref,
    high_ref,
    piece_ref,
):
    groups = node_ref.shape[0]
    steps = groups // SUB
    own = low_ref.shape[0]
    nodes3 = f3_ref.shape[0]
    nodes4 = f4_ref.shape[0]
    tag_count = 2 * nodes4
    piece_ref[...] = jnp.zeros_like(piece_ref)

    def code_start(feature):
        return (feature // SUB) * (groups * SUB) + feature % SUB

    def code_block(start, step):
        return codes_ref[pl.ds(start + step * (SUB * SUB), SUB, stride=SUB), :]

    def goes_right(nodes, feature_ref, bin_ref):
        margin = [jnp.zeros((SUB, LANES), jnp.int32) for _ in nodes]
        for n in range(feature_ref.shape[0]):
            start = code_start(feature_ref[n])
            cut = bin_ref[n]
            for step, node in enumerate(nodes):
                margin[step] = jnp.where(node == n, code_block(start, step) - cut, margin[step])
        return [jnp.where(m > 0, 1, 0) for m in margin]

    def rows_of(step):
        return slice(step * SUB, (step + 1) * SUB)

    node3 = [node_ref[rows_of(step), :] for step in range(steps)]
    right3 = goes_right(node3, f3_ref, b3_ref)
    node4 = [2 * n + r for n, r in zip(node3, right3)]
    right4 = goes_right(node4, f4_ref, b4_ref)
    first = lax.axis_index("feat") * own
    starts = [code_start(first + i) for i in range(own)]
    for step in range(steps):
        rows = rows_of(step)
        positive = jnp.where(label_ref[rows, :] > 0, 1, 0)
        tag = right3[step] * (2 * nodes3) + positive * nodes3 + node3[step]
        path_ref[rows, :] = right4[step] * tag_count + tag
        for i in range(own):
            code = code_block(starts[i], step)
            low_ref[i, rows, :] = code & (LANES - 1)
            slot_ref[i, rows, :] = (code // LANES) * tag_count + tag
        weight = weight_ref[rows, :]
        high = weight.astype(jnp.bfloat16).astype(jnp.float32)
        mid = (weight - high).astype(jnp.bfloat16).astype(jnp.float32)
        high_ref[rows, :] = high
        for k, piece in enumerate((high, mid, weight - high - mid)):
            for side in range(2):
                spots = pl.ds(step * (SUB * SUB) + 2 * k + side, SUB, stride=SUB)
                piece_ref[spots, :] = jnp.where(right4[step] == side, piece, 0.0)

    cell = (2 * SUB, LANES)
    iota = lax.broadcasted_iota(jnp.int32, cell, 0)
    small = jnp.int16
    ranks = [(iota + 2 * SUB * g).astype(small) for g in range(LANES // (2 * SUB))]
    one = jnp.ones(cell, jnp.bfloat16)
    nothing = jnp.zeros(cell, jnp.bfloat16)
    def spread(ref, row, dtype, *lead):
        line = ref[(*lead, pl.ds(row, 1), slice(None))]
        return jnp.broadcast_to(line, cell).astype(dtype)

    def onehot(value, count, filled):
        parts = [jnp.where(value == ranks[g], filled, nothing) for g in range(count // (2 * SUB))]
        return jnp.concatenate(parts, axis=0)

    halves = DEPTH // LANES
    tiles = groups // halves
    units = 2

    def fill(tile):
        lines = range(tile * halves, (tile + 1) * halves)
        columns = [
            jnp.concatenate(
                [
                    onehot(spread(slot_ref, line, small, i), 2 * tag_count, one)
                    for i in range(own)
                ],
                axis=0,
            )
            for line in lines
        ]
        pltpu.matmul_push_rhs(
            jnp.concatenate(columns, axis=1), tile // units % 2, tile % units, transpose=True
        )

    def stream(tile, accs):
        columns = []
        for line in range(tile * halves, (tile + 1) * halves):
            heavy = spread(high_ref, line, jnp.bfloat16)
            parts = [onehot(spread(low_ref, line, small, i), LANES, heavy) for i in range(own)]
            pieces = piece_ref[line * SUB : (line + 1) * SUB, :]
            parts.append(
                jnp.concatenate([pieces, jnp.zeros_like(pieces)], axis=0).astype(jnp.bfloat16)
            )
            columns.append(jnp.concatenate(parts, axis=0))
        pltpu.matmul_acc_lhs(
            accs[tile % units], jnp.concatenate(columns, axis=1), tile // units % 2
        )

    def product(*accs):
        for tile in range(units):
            fill(tile)
        for tile in range(tiles):
            if tile + units < tiles:
                fill(tile + units)
            stream(tile, accs)
        return pltpu.matmul_pop(accs[0]) + pltpu.matmul_pop(accs[1])

    shape = (own * LANES + 2 * SUB, DEPTH)
    sums = pl.run_scoped(
        product, *(pltpu.ACC(unit)(shape, jnp.float32) for unit in range(units))
    )
    left = lax.broadcasted_iota(jnp.int32, (LANES, LANES), 1) < 2 * tag_count
    for pair in range(own // 2):
        lanes = slice(pair * LANES, (pair + 1) * LANES)
        rows = [slice(i * LANES, (i + 1) * LANES) for i in (2 * pair, 2 * pair + 1)]
        hist_ref[lanes, :] = jnp.where(left, sums[rows[0], lanes], sums[rows[1], lanes])
    doubled = sums[own * LANES : own * LANES + SUB, 0:LANES]
    hist_ref[own // 2 * LANES : own // 2 * LANES + SUB, :] = doubled + pltpu.roll(
        doubled, LANES - tag_count, 1
    )


def finish_kernel(
    total,
    hist_ref,
    path_ref,
    weight_ref,
    score_ref,
    hist3_ref,
    hist4_ref,
    value_ref,
    new_score_ref,
    new_weight_ref,
    weave_ref,
):
    own, tags, _ = hist4_ref.shape
    nodes4 = tags // 2
    nodes3 = nodes4 // 2
    leaves = value_ref.shape[1]
    for pair in range(own // 2):
        turned = hist_ref[pair * LANES : (pair + 1) * LANES, :].T
        for q in range(4):
            i = 2 * pair + q // 2
            h = q % 2
            lanes = slice(h * LANES, (h + 1) * LANES)
            start = q * tags
            keep = (pair * 4 + q) * tags

            def tag_rows(right, positive):
                first = start + right * 2 * nodes3 + positive * nodes3
                return turned[first : first + nodes3, :]

            sums = [tag_rows(r, 1) + tag_rows(r, 0) for r in range(2)]
            diffs = [tag_rows(r, 1) - tag_rows(r, 0) for r in range(2)]
            hist3_ref[i, 0:nodes3, lanes] = sums[0] + sums[1]
            hist3_ref[i, nodes3 : 2 * nodes3, lanes] = diffs[0] + diffs[1]
            for r in range(2):
                weave_ref[pl.ds(keep + r, nodes3, stride=2), :] = sums[r]
                weave_ref[pl.ds(keep + nodes4 + r, nodes3, stride=2), :] = diffs[r]
            hist4_ref[i, :, lanes] = weave_ref[keep : keep + tags, :]
    leaf_base = own // 2 * LANES
    pieces = hist_ref[leaf_base : leaf_base + SUB, :]
    lane = lax.broadcasted_iota(jnp.int32, (1, LANES), 1)
    right = (lane & tags) > 0
    positive = (lane & nodes3) > 0

    def both_sides(k):
        return jnp.where(
            right, pltpu.roll(pieces[2 * k + 1 : 2 * k + 2, :], tags, 1), pieces[2 * k : 2 * k + 1, :]
        )

    def partner(line):
        return jnp.where(
            positive, pltpu.roll(line, nodes3, 1), pltpu.roll(line, LANES - nodes3, 1)
        )

    rounded = both_sides(0)
    full = rounded + (both_sides(1) + both_sides(2))
    inside = lane < 2 * tags
    other = partner(rounded)
    gap = jnp.where(positive, rounded - other, other - rounded)
    values = jnp.where(inside, gap / (rounded + other + 1.0), 0.0)
    growth = jnp.exp(jnp.where(positive, -values, values))
    grand = jnp.sum(jnp.where(inside, full * growth, 0.0), axis=1, keepdims=True)
    factor = growth * (total / grand)
    factor8 = jnp.broadcast_to(factor, (SUB, LANES))
    both8 = jnp.broadcast_to(values, (SUB, LANES))
    leaf = lax.broadcasted_iota(jnp.int32, (SUB, LANES), 1)
    spot = (leaf & 1) * tags + ((leaf >> 1) & 1) * (2 * nodes3) + ((leaf >> 2) & (nodes3 - 1))
    value_ref[...] = jnp.take_along_axis(both8, spot, axis=1)[0:1, 0:leaves]
    for step in range(path_ref.shape[0] // SUB):
        rows = slice(step * SUB, (step + 1) * SUB)
        path = path_ref[rows, :]
        scale = jnp.take_along_axis(factor8, path, axis=1)
        shift = jnp.take_along_axis(both8, path, axis=1)
        new_weight_ref[rows, :] = weight_ref[rows, :] * scale
        new_score_ref[rows, :] = score_ref[rows, :] + shift


def combine_rows(part, row_parts, feat_parts):
    if row_parts & (row_parts - 1):
        return lax.psum(part, "rows")
    bits = row_parts.bit_length() - 1
    for step in range(bits):
        pairs = []
        for row in range(row_parts):
            for feat in range(feat_parts):
                other = row ^ reach(feat, step, bits)
                pairs.append((row * feat_parts + feat, other * feat_parts + feat))
        part = part + lax.ppermute(part, ("rows", "feat"), pairs)
    return part


def reach(feat, step, bits):
    return 1 << (step + feat % 2 * (bits - 1)) % bits


def whole(memory=pltpu.VMEM):
    return pl.BlockSpec(memory_space=memory)


def on_device(
    row_parts,
    feat_parts,
    bin_codes,
    node_ids,
    labels,
    weights,
    predictions,
    level3_feature,
    level3_bin,
    level4_feature,
    level4_bin,
):
    features, row_count = bin_codes.shape
    groups = row_count // LANES
    own = features // feat_parts
    nodes3 = level3_feature.shape[0]
    nodes4 = level4_feature.shape[0]
    leaves = 2 * nodes4
    tags = 2 * nodes4
    codes = (
        bin_codes.reshape(features // SUB, SUB, groups, LANES)
        .transpose(0, 2, 1, 3)
        .reshape(features * groups, LANES)
    )
    square = (groups, LANES)
    node_sq = node_ids.reshape(square)
    label_sq = labels.reshape(square)
    weight_sq = weights.reshape(square)
    score_sq = predictions.reshape(square)
    hist_rows = own // 2 * LANES + SUB
    f32, i32 = jnp.float32, jnp.int32
    held = functools.partial(pltpu.with_memory_space_constraint, memory_space=pltpu.HBM)
    hist, path = pl.pallas_call(
        grow_kernel,
        out_shape=(pltpu.VMEM((hist_rows, LANES), f32), pltpu.VMEM(square, i32)),
        in_specs=[whole(pltpu.SMEM)] * 4 + [whole()] * 4,
        out_specs=(whole(), whole()),
        scratch_shapes=[
            pltpu.VMEM((own, *square), i32),
            pltpu.VMEM((own, *square), i32),
            pltpu.VMEM(square, f32),
            pltpu.VMEM((groups * SUB, LANES), f32),
        ],
        compiler_params=pltpu.CompilerParams(vmem_limit_bytes=24 * 1024 * 1024),
    )(
        held(level3_feature),
        held(level3_bin),
        held(level4_feature),
        held(level4_bin),
        held(codes),
        held(node_sq),
        held(label_sq),
        held(weight_sq),
    )
    hist = combine_rows(hist, row_parts, feat_parts)
    hist3, hist4, values, new_scores, new_weights = pl.pallas_call(
        functools.partial(finish_kernel, float(row_count * row_parts)),
        out_shape=(
            jax.ShapeDtypeStruct((own, 2 * nodes3, BINS), f32),
            jax.ShapeDtypeStruct((own, 2 * nodes4, BINS), f32),
            jax.ShapeDtypeStruct((1, leaves), f32),
            jax.ShapeDtypeStruct(square, f32),
            jax.ShapeDtypeStruct(square, f32),
        ),
        in_specs=[whole()] * 4,
        out_specs=(whole(),) * 5,
        scratch_shapes=[pltpu.VMEM((own * 2 * tags, LANES), f32)],
        compiler_params=pltpu.CompilerParams(vmem_limit_bytes=24 * 1024 * 1024),
    )(hist, path, weight_sq, score_sq)
    return (
        hist3,
        hist4,
        values.reshape(leaves),
        new_scores.reshape(row_count),
        new_weights.reshape(row_count),
    )


def solution(mesh):
    placed = (P(None, "rows"), P("rows"), P("rows"), P("rows"), P("rows"), P(), P(), P(), P())
    return jax.shard_map(
        functools.partial(on_device, mesh.shape["rows"], mesh.shape["feat"]),
        mesh=mesh,
        in_specs=placed,
        out_specs=(P("feat", None, None), P("feat", None, None), P(), P("rows"), P("rows")),
        check_vma=False,
    )
```

```python
import functools

import jax
import jax.numpy as jnp
from jax import lax
from jax.experimental import pallas as pl
from jax.experimental.pallas import tpu as pltpu
from jax.sharding import PartitionSpec as P

BINS = 256
LANES = 128
SUB = 8
DEPTH = 256
NT = (((1,), (1,)), ((), ()))


def grow_kernel(
    f3_ref,
    b3_ref,
    f4_ref,
    b4_ref,
    codes_ref,
    node_ref,
    label_ref,
    weight_ref,
    hist_ref,
    path_ref,
    low_ref,
    slot_ref,
    high_ref,
    piece_ref,
):
    groups = node_ref.shape[0]
    steps = groups // SUB
    own = low_ref.shape[0]
    nodes3 = f3_ref.shape[0]
    nodes4 = f4_ref.shape[0]
    tag_count = 2 * nodes4
    piece_ref[...] = jnp.zeros_like(piece_ref)

    def code_start(feature):
        return (feature // SUB) * (groups * SUB) + feature % SUB

    def code_block(start, step):
        return codes_ref[pl.ds(start + step * (SUB * SUB), SUB, stride=SUB), :]

    def goes_right(nodes, feature_ref, bin_ref):
        margin = [jnp.zeros((SUB, LANES), jnp.int32) for _ in nodes]
        for n in range(feature_ref.shape[0]):
            start = code_start(feature_ref[n])
            cut = bin_ref[n]
            for step, node in enumerate(nodes):
                margin[step] = jnp.where(node == n, code_block(start, step) - cut, margin[step])
        return [jnp.where(m > 0, 1, 0) for m in margin]

    def rows_of(step):
        return slice(step * SUB, (step + 1) * SUB)

    node3 = [node_ref[rows_of(step), :] for step in range(steps)]
    right3 = goes_right(node3, f3_ref, b3_ref)
    node4 = [2 * n + r for n, r in zip(node3, right3)]
    right4 = goes_right(node4, f4_ref, b4_ref)
    first = lax.axis_index("feat") * own
    starts = [code_start(first + i) for i in range(own)]
    for step in range(steps):
        rows = rows_of(step)
        positive = jnp.where(label_ref[rows, :] > 0, 1, 0)
        tag = right3[step] * (2 * nodes3) + positive * nodes3 + node3[step]
        path_ref[rows, :] = right4[step] * tag_count + tag
        for i in range(own):
            code = code_block(starts[i], step)
            low_ref[i, rows, :] = code & (LANES - 1)
            slot_ref[i, rows, :] = (code // LANES) * tag_count + tag
        weight = weight_ref[rows, :]
        high = weight.astype(jnp.bfloat16).astype(jnp.float32)
        mid = (weight - high).astype(jnp.bfloat16).astype(jnp.float32)
        high_ref[rows, :] = high
        for k, piece in enumerate((high, mid, weight - high - mid)):
            for side in range(2):
                spots = pl.ds(step * (SUB * SUB) + 2 * k + side, SUB, stride=SUB)
                piece_ref[spots, :] = jnp.where(right4[step] == side, piece, 0.0)

    cell = (2 * SUB, LANES)
    iota = lax.broadcasted_iota(jnp.int32, cell, 0)
    small = jnp.int16
    ranks = [(iota + 2 * SUB * g).astype(small) for g in range(LANES // (2 * SUB))]
    one = jnp.ones(cell, jnp.bfloat16)
    nothing = jnp.zeros(cell, jnp.bfloat16)
    def spread(ref, row, dtype, *lead):
        line = ref[(*lead, pl.ds(row, 1), slice(None))]
        return jnp.broadcast_to(line, cell).astype(dtype)

    def onehot(value, count, filled):
        parts = [jnp.where(value == ranks[g], filled, nothing) for g in range(count // (2 * SUB))]
        return jnp.concatenate(parts, axis=0)

    halves = DEPTH // LANES
    tiles = groups // halves
    units = 2

    def fill(tile):
        lines = range(tile * halves, (tile + 1) * halves)
        columns = [
            jnp.concatenate(
                [
                    onehot(spread(slot_ref, line, small, i), 2 * tag_count, one)
                    for i in range(own)
                ],
                axis=0,
            )
            for line in lines
        ]
        pltpu.matmul_push_rhs(
            jnp.concatenate(columns, axis=1), tile // units % 2, tile % units, transpose=True
        )

    def stream(tile, accs):
        columns = []
        for line in range(tile * halves, (tile + 1) * halves):
            heavy = spread(high_ref, line, jnp.bfloat16)
            parts = [onehot(spread(low_ref, line, small, i), LANES, heavy) for i in range(own)]
            pieces = piece_ref[line * SUB : (line + 1) * SUB, :]
            parts.append(
                jnp.concatenate([pieces, jnp.zeros_like(pieces)], axis=0).astype(jnp.bfloat16)
            )
            columns.append(jnp.concatenate(parts, axis=0))
        pltpu.matmul_acc_lhs(
            accs[tile % units], jnp.concatenate(columns, axis=1), tile // units % 2
        )

    def product(*accs):
        for tile in range(units):
            fill(tile)
        for tile in range(tiles):
            if tile + units < tiles:
                fill(tile + units)
            stream(tile, accs)
        return pltpu.matmul_pop(accs[0]) + pltpu.matmul_pop(accs[1])

    shape = (own * LANES + 2 * SUB, DEPTH)
    sums = pl.run_scoped(
        product, *(pltpu.ACC(unit)(shape, jnp.float32) for unit in range(units))
    )
    left = lax.broadcasted_iota(jnp.int32, (LANES, LANES), 1) < 2 * tag_count
    for pair in range(own // 2):
        lanes = slice(pair * LANES, (pair + 1) * LANES)
        rows = [slice(i * LANES, (i + 1) * LANES) for i in (2 * pair, 2 * pair + 1)]
        hist_ref[lanes, :] = jnp.where(left, sums[rows[0], lanes], sums[rows[1], lanes])
    doubled = sums[own * LANES : own * LANES + SUB, 0:LANES]
    hist_ref[own // 2 * LANES : own // 2 * LANES + SUB, :] = doubled + pltpu.roll(
        doubled, LANES - tag_count, 1
    )


def finish_kernel(
    total,
    part_ref,
    received_ref,
    path_ref,
    weight_ref,
    score_ref,
    hist3_ref,
    hist4_ref,
    value_ref,
    new_score_ref,
    new_weight_ref,
    weave_ref,
):
    own, tags, _ = hist4_ref.shape
    nodes4 = tags // 2
    nodes3 = nodes4 // 2
    leaves = value_ref.shape[1]

    def hist_rows(first, count):
        rows = slice(first, first + count)
        return part_ref[rows, :] + received_ref[rows, :]

    for pair in range(own // 2):
        turned = hist_rows(pair * LANES, LANES).T
        for q in range(4):
            i = 2 * pair + q // 2
            h = q % 2
            lanes = slice(h * LANES, (h + 1) * LANES)
            start = q * tags
            keep = (pair * 4 + q) * tags

            def tag_rows(right, positive):
                first = start + right * 2 * nodes3 + positive * nodes3
                return turned[first : first + nodes3, :]

            sums = [tag_rows(r, 1) + tag_rows(r, 0) for r in range(2)]
            diffs = [tag_rows(r, 1) - tag_rows(r, 0) for r in range(2)]
            hist3_ref[i, 0:nodes3, lanes] = sums[0] + sums[1]
            hist3_ref[i, nodes3 : 2 * nodes3, lanes] = diffs[0] + diffs[1]
            for r in range(2):
                weave_ref[pl.ds(keep + r, nodes3, stride=2), :] = sums[r]
                weave_ref[pl.ds(keep + nodes4 + r, nodes3, stride=2), :] = diffs[r]
            hist4_ref[i, :, lanes] = weave_ref[keep : keep + tags, :]
    leaf_base = own // 2 * LANES
    pieces = hist_rows(leaf_base, SUB)
    lane = lax.broadcasted_iota(jnp.int32, (1, LANES), 1)
    right = (lane & tags) > 0
    positive = (lane & nodes3) > 0

    def both_sides(k):
        return jnp.where(
            right, pltpu.roll(pieces[2 * k + 1 : 2 * k + 2, :], tags, 1), pieces[2 * k : 2 * k + 1, :]
        )

    def partner(line):
        return jnp.where(
            positive, pltpu.roll(line, nodes3, 1), pltpu.roll(line, LANES - nodes3, 1)
        )

    rounded = both_sides(0)
    full = rounded + (both_sides(1) + both_sides(2))
    inside = lane < 2 * tags
    other = partner(rounded)
    gap = jnp.where(positive, rounded - other, other - rounded)
    values = jnp.where(inside, gap / (rounded + other + 1.0), 0.0)
    growth = jnp.exp(jnp.where(positive, -values, values))
    grand = jnp.sum(jnp.where(inside, full * growth, 0.0), axis=1, keepdims=True)
    factor = growth * (total / grand)
    factor8 = jnp.broadcast_to(factor, (SUB, LANES))
    both8 = jnp.broadcast_to(values, (SUB, LANES))
    leaf = lax.broadcasted_iota(jnp.int32, (SUB, LANES), 1)
    spot = (leaf & 1) * tags + ((leaf >> 1) & 1) * (2 * nodes3) + ((leaf >> 2) & (nodes3 - 1))
    value_ref[...] = jnp.take_along_axis(both8, spot, axis=1)[0:1, 0:leaves]
    for step in range(path_ref.shape[0] // SUB):
        rows = slice(step * SUB, (step + 1) * SUB)
        path = path_ref[rows, :]
        scale = jnp.take_along_axis(factor8, path, axis=1)
        shift = jnp.take_along_axis(both8, path, axis=1)
        new_weight_ref[rows, :] = weight_ref[rows, :] * scale
        new_score_ref[rows, :] = score_ref[rows, :] + shift


def combine_rows(part, row_parts, feat_parts):
    if row_parts & (row_parts - 1):
        return lax.psum(part, "rows"), jnp.zeros_like(part)
    bits = row_parts.bit_length() - 1
    for step in range(bits):
        pairs = []
        for row in range(row_parts):
            for feat in range(feat_parts):
                other = row ^ reach(feat, step, bits)
                pairs.append((row * feat_parts + feat, other * feat_parts + feat))
        received = lax.ppermute(part, ("rows", "feat"), pairs)
        if step == bits - 1:
            return part, received
        part = part + received
    return part, jnp.zeros_like(part)


def reach(feat, step, bits):
    return 1 << (step + feat % 2 * (bits - 1)) % bits


def whole(memory=pltpu.VMEM):
    return pl.BlockSpec(memory_space=memory)


def on_device(
    row_parts,
    feat_parts,
    bin_codes,
    node_ids,
    labels,
    weights,
    predictions,
    level3_feature,
    level3_bin,
    level4_feature,
    level4_bin,
):
    features, row_count = bin_codes.shape
    groups = row_count // LANES
    own = features // feat_parts
    nodes3 = level3_feature.shape[0]
    nodes4 = level4_feature.shape[0]
    leaves = 2 * nodes4
    tags = 2 * nodes4
    codes = (
        bin_codes.reshape(features // SUB, SUB, groups, LANES)
        .transpose(0, 2, 1, 3)
        .reshape(features * groups, LANES)
    )
    square = (groups, LANES)
    node_sq = node_ids.reshape(square)
    label_sq = labels.reshape(square)
    weight_sq = weights.reshape(square)
    score_sq = predictions.reshape(square)
    hist_rows = own // 2 * LANES + SUB
    f32, i32 = jnp.float32, jnp.int32
    held = functools.partial(pltpu.with_memory_space_constraint, memory_space=pltpu.HBM)
    hist, path = pl.pallas_call(
        grow_kernel,
        out_shape=(pltpu.VMEM((hist_rows, LANES), f32), pltpu.VMEM(square, i32)),
        in_specs=[whole(pltpu.SMEM)] * 4 + [whole()] * 4,
        out_specs=(whole(), whole()),
        scratch_shapes=[
            pltpu.VMEM((own, *square), i32),
            pltpu.VMEM((own, *square), i32),
            pltpu.VMEM(square, f32),
            pltpu.VMEM((groups * SUB, LANES), f32),
        ],
        compiler_params=pltpu.CompilerParams(vmem_limit_bytes=24 * 1024 * 1024),
    )(
        held(level3_feature),
        held(level3_bin),
        held(level4_feature),
        held(level4_bin),
        held(codes),
        held(node_sq),
        held(label_sq),
        held(weight_sq),
    )
    hist, received = combine_rows(hist, row_parts, feat_parts)
    hist3, hist4, values, new_scores, new_weights = pl.pallas_call(
        functools.partial(finish_kernel, float(row_count * row_parts)),
        out_shape=(
            jax.ShapeDtypeStruct((own, 2 * nodes3, BINS), f32),
            jax.ShapeDtypeStruct((own, 2 * nodes4, BINS), f32),
            jax.ShapeDtypeStruct((1, leaves), f32),
            jax.ShapeDtypeStruct(square, f32),
            jax.ShapeDtypeStruct(square, f32),
        ),
        in_specs=[whole()] * 5,
        out_specs=(whole(),) * 5,
        scratch_shapes=[pltpu.VMEM((own * 2 * tags, LANES), f32)],
        compiler_params=pltpu.CompilerParams(vmem_limit_bytes=24 * 1024 * 1024),
    )(hist, received, path, weight_sq, score_sq)
    return (
        hist3,
        hist4,
        values.reshape(leaves),
        new_scores.reshape(row_count),
        new_weights.reshape(row_count),
    )


def solution(mesh):
    placed = (P(None, "rows"), P("rows"), P("rows"), P("rows"), P("rows"), P(), P(), P(), P())
    return jax.shard_map(
        functools.partial(on_device, mesh.shape["rows"], mesh.shape["feat"]),
        mesh=mesh,
        in_specs=placed,
        out_specs=(P("feat", None, None), P("feat", None, None), P(), P("rows"), P("rows")),
        check_vma=False,
    )
```
